32 devices in a mesh: groups: 2 (over y), heads: 8 (over z, x), width: 2 (over core).
Axes of the slice: x: 2, y: 2, z: 4, core: 2. Of those that a mesh axis runs over, the one named last changes fastest.
Arguments:
- tokens: bfloat16 [768, 16384], P(('groups', 'heads'), 'width'), parts along dimension 0, may hold values from -20 to 20
- norm_gain: bfloat16 [16384], P('width'), may hold values from 0.4 to 12
- w_query: bfloat16 [16384, 16384], P('width', 'heads'), may hold values from -0.046875 to 0.046875
- key_weight_matrix: bfloat16 [16384, 1024], P('width', 'heads'), may hold values from -0.046875 to 0.046875
- value_weight_matrix: bfloat16 [16384, 1024], P('width', 'heads'), may hold values from -0.046875 to 0.046875
- w_out: bfloat16 [16384, 16384], P('width', 'heads'), may hold values from -0.046875 to 0.046875
- prompt_len: int32 [4], P('groups'), parts along dimension 0, may hold values from 48 to 192
- prefix_len: int32 [4], P('groups'), parts along dimension 0, may hold values from 1 to 96
Outputs:
- block_out: bfloat16 [768, 16384], P(('groups', 'width'), 'heads'), parts along dimension 0
The draws below stay inside these ranges and needn't reach their ends.
There are 2 independent parts, one for each index of `groups`. The reference program is written for one: setup_inputs(seed, part) draws one part's arguments, and reference() takes and returns one part's arrays. A program takes and returns all parts, laid end to end along the dimension named above; an argument that names none is the same for every part. Nothing has to cross between parts.
All inputs are finite; a program needn't handle non-finite values.
Results may differ from the reference program's by a relative error of at most 0.005.
The reference program's roundings to bfloat16 on the way count: a program that leaves them out, or rounds other values in their place, can miss the bound.
Values may be sent and summed in bfloat16 or wider, within the bound.
A program may use at most 320 MiB of HBM per device.

```python
import math
import jax
import jax.numpy as jnp
from jax import lax

MODEL_WIDTH = 16384
QUERY_HEADS = 128
KEY_VALUE_HEADS = 8
HEAD_WIDTH = 128
PROMPT_SLOTS = 192
GROUP_PROMPTS = 2
TOKENS = 384


def draw_tokens(key, part):
    key = jax.random.fold_in(key, 11)
    noise_key, column_key, row_key = jax.random.split(key, 3)
    column_scale = jnp.exp(jax.random.uniform(column_key, (1, MODEL_WIDTH), jnp.float32, jnp.log(0.25), jnp.log(2.5)))
    row_scale = jnp.exp(jax.random.uniform(row_key, (TOKENS, 1), jnp.float32, jnp.log(0.5), jnp.log(2.0)))
    pattern = jnp.clip(jax.random.normal(noise_key, (TOKENS, MODEL_WIDTH), jnp.float32), -4.0, 4.0)
    return jnp.clip(pattern * column_scale * row_scale, -20.0, 20.0).astype(jnp.bfloat16)


def draw_norm_gain(key, part):
    key = jax.random.fold_in(key, 12)
    gains = jnp.exp(jax.random.uniform(key, (MODEL_WIDTH,), jnp.float32, jnp.log(0.4), jnp.log(2.5)))
    return gains.astype(jnp.bfloat16)


def block_levels(own_key, shape, cuts, low, largest):
    loudness = 1.0
    for axis_at, blocks in cuts:
        steps = jax.random.uniform(jax.random.fold_in(jax.random.fold_in(own_key, 6), axis_at), (blocks,), jnp.float32, low / len(cuts), largest / len(cuts))
        loudness = loudness * jnp.repeat(jnp.exp(steps), shape[axis_at] // blocks).reshape((-1,) + (1,) * (len(shape) - 1 - axis_at))
    return loudness


def scatter_about(own_key, extent, width, bound, shards=(), kind=jnp.bfloat16):
    values = width * jax.random.normal(own_key, extent, jnp.float32)
    if shards:
        values = values * block_levels(own_key, extent, shards, -0.22, 0.18)
    return jnp.clip(values, -bound, bound).astype(kind)


def setup_inputs(seed: int = 0, part: int = 0) -> dict:
    key_of = jax.random.split(jax.random.key(seed), 9)
    part_keys = jax.random.split(jax.random.fold_in(key_of[8], part), 9)
    tokens = draw_tokens(jax.random.fold_in(jax.random.fold_in(key_of[8], part), 71), part)
    norm_gain = draw_norm_gain(jax.random.fold_in(key_of[8], 71), part)
    w_query = scatter_about(key_of[2], (MODEL_WIDTH, QUERY_HEADS * HEAD_WIDTH), MODEL_WIDTH ** -0.5, 0.046875, ((0, 2), (1, 8)))
    key_weight_matrix = scatter_about(key_of[3], (MODEL_WIDTH, KEY_VALUE_HEADS * HEAD_WIDTH), MODEL_WIDTH ** -0.5, 0.046875, ((0, 2), (1, 8)))
    value_weight_matrix = scatter_about(key_of[4], (MODEL_WIDTH, KEY_VALUE_HEADS * HEAD_WIDTH), MODEL_WIDTH ** -0.5, 0.046875, ((0, 2), (1, 8)))
    w_out = scatter_about(key_of[5], (QUERY_HEADS * HEAD_WIDTH, MODEL_WIDTH), (QUERY_HEADS * HEAD_WIDTH) ** -0.5, 0.046875, ((0, 2), (1, 8)))
    prompt_len = jax.random.randint(part_keys[6], (GROUP_PROMPTS,), PROMPT_SLOTS // 4, PROMPT_SLOTS + 1).astype(jnp.int32)
    prefix_len = jax.random.randint(part_keys[7], (GROUP_PROMPTS,), 1, PROMPT_SLOTS // 2 + 1).astype(jnp.int32)
    return dict(tokens=tokens, norm_gain=norm_gain, w_query=w_query, key_weight_matrix=key_weight_matrix, value_weight_matrix=value_weight_matrix, w_out=w_out, prompt_len=prompt_len, prefix_len=prefix_len)


def rope_angles(length, head_size):
    half_size = head_size // 2
    indices = jnp.arange(half_size, dtype=jnp.float32)
    frequency = jnp.exp(-(2.0 * indices / head_size) * math.log(500000.0))
    wavelength = 2.0 * math.pi / frequency
    smooth = (8192.0 / wavelength - 1.0) / 3.0
    blended = (1.0 - smooth) * frequency / 8.0 + smooth * frequency
    frequency = jnp.where(wavelength < 2048.0, frequency, jnp.where(wavelength > 8192.0, frequency / 8.0, blended))
    positions = jnp.arange(length, dtype=jnp.float32)
    angles = positions[:, None] * frequency[None, :]
    return (jnp.cos(angles), jnp.sin(angles))

def rotate(vectors, cosine_table, sine_table):
    half_size = vectors.shape[-1] // 2
    leading = vectors[..., :half_size]
    trailing = vectors[..., half_size:]
    cosine_wide = cosine_table[:, None, :]
    sine_wide = sine_table[:, None, :]
    return jnp.concatenate([leading * cosine_wide - trailing * sine_wide, trailing * cosine_wide + leading * sine_wide], axis=-1)

def allowed_mask(length, prompt_length, prefix_length):
    query_slot = jnp.arange(length, dtype=jnp.int32)[:, None]
    key_slot = jnp.arange(length, dtype=jnp.int32)[None, :]
    return (key_slot < prompt_length) & ((key_slot <= query_slot) | (key_slot < prefix_length))

def reference(tokens, norm_gain, w_query, key_weight_matrix, value_weight_matrix, w_out, prompt_len, prefix_len):
    widened = tokens.astype(jnp.float32)
    mean_square = lax.optimization_barrier(jnp.sum(widened * widened, axis=1, keepdims=True)) / MODEL_WIDTH
    normed_inputs = (widened * lax.rsqrt(mean_square + 1e-05) * norm_gain.astype(jnp.float32)[None, :]).astype(jnp.bfloat16)
    cosine_table, sine_table = rope_angles(PROMPT_SLOTS, HEAD_WIDTH)
    queries_raw = jnp.dot(normed_inputs, w_query, preferred_element_type=jnp.float32).reshape(GROUP_PROMPTS, PROMPT_SLOTS, QUERY_HEADS, HEAD_WIDTH)
    queries = rotate(queries_raw, cosine_table, sine_table).astype(jnp.bfloat16)
    unrotated_keys = jnp.dot(normed_inputs, key_weight_matrix, preferred_element_type=jnp.float32).astype(jnp.bfloat16).reshape(GROUP_PROMPTS, PROMPT_SLOTS, HEAD_WIDTH, KEY_VALUE_HEADS)
    unrotated_keys = jnp.swapaxes(unrotated_keys, 2, 3)
    rotated_keys = rotate(unrotated_keys.astype(jnp.float32), cosine_table, sine_table).astype(jnp.bfloat16)
    value_vectors = jnp.dot(normed_inputs, value_weight_matrix, preferred_element_type=jnp.float32).astype(jnp.bfloat16).reshape(GROUP_PROMPTS, PROMPT_SLOTS, HEAD_WIDTH, KEY_VALUE_HEADS)
    value_vectors = jnp.swapaxes(value_vectors, 2, 3)
    heads_per_group = QUERY_HEADS // KEY_VALUE_HEADS

    def one_prompt(inputs):
        query_tile_rows, key_block, value_block, length_one, prefix_one = inputs
        grouped_queries = query_tile_rows.reshape(PROMPT_SLOTS, KEY_VALUE_HEADS, heads_per_group, HEAD_WIDTH).astype(jnp.float32)
        scores = jnp.einsum('qngd,knd->ngqk', grouped_queries, key_block.astype(jnp.float32)) / math.sqrt(HEAD_WIDTH)
        allowed = allowed_mask(PROMPT_SLOTS, length_one, prefix_one)
        scores = jnp.where(allowed[None, None], scores, jnp.float32(-1e+30))
        row_peak = lax.optimization_barrier(jnp.max(scores, axis=-1, keepdims=True))
        raised = jnp.exp(scores - row_peak)
        probabilities = (raised / lax.optimization_barrier(jnp.sum(raised, axis=-1, keepdims=True))).astype(jnp.bfloat16)
        mixture = jnp.einsum('ngqk,knd->qngd', probabilities.astype(jnp.float32), value_block.astype(jnp.float32))
        return mixture.astype(jnp.bfloat16).reshape(PROMPT_SLOTS, QUERY_HEADS * HEAD_WIDTH)
    attended = lax.map(one_prompt, (queries, rotated_keys, value_vectors, prompt_len, prefix_len))
    attended = attended.reshape(GROUP_PROMPTS * PROMPT_SLOTS, QUERY_HEADS * HEAD_WIDTH)
    return jnp.dot(attended, w_out, preferred_element_type=jnp.float32).astype(jnp.bfloat16)
```

```python
import math

import jax
import jax.numpy as jnp
from jax import lax
from jax.sharding import PartitionSpec as P

MODEL_WIDTH = 16384
QUERY_HEADS = 128
KEY_VALUE_HEADS = 8
HEAD_WIDTH = 128
PROMPT_SLOTS = 192


def rope_angles(length, head_size):
    half_size = head_size // 2
    indices = jnp.arange(half_size, dtype=jnp.float32)
    frequency = jnp.exp(-(2.0 * indices / head_size) * math.log(500000.0))
    wavelength = 2.0 * math.pi / frequency
    smooth = (8192.0 / wavelength - 1.0) / 3.0
    blended = (1.0 - smooth) * frequency / 8.0 + smooth * frequency
    frequency = jnp.where(
        wavelength < 2048.0, frequency, jnp.where(wavelength > 8192.0, frequency / 8.0, blended)
    )
    positions = jnp.arange(length, dtype=jnp.float32)
    angles = positions[:, None] * frequency[None, :]
    return (jnp.cos(angles), jnp.sin(angles))


def rotate(vectors, cosine_table, sine_table):
    half_size = vectors.shape[-1] // 2
    leading = vectors[..., :half_size]
    trailing = vectors[..., half_size:]
    cosine_wide = cosine_table[:, None, :]
    sine_wide = sine_table[:, None, :]
    return jnp.concatenate(
        [
            leading * cosine_wide - trailing * sine_wide,
            trailing * cosine_wide + leading * sine_wide,
        ],
        axis=-1,
    )


def allowed_mask(length, prompt_length, prefix_length):
    query_slot = jnp.arange(length, dtype=jnp.int32)[:, None]
    key_slot = jnp.arange(length, dtype=jnp.int32)[None, :]
    return (key_slot < prompt_length) & ((key_slot <= query_slot) | (key_slot < prefix_length))


def per_device(
    tokens,
    norm_gain,
    w_query,
    key_weight_matrix,
    value_weight_matrix,
    w_out,
    prompt_len,
    prefix_len,
):
    head_count = lax.axis_size("heads")
    width_count = lax.axis_size("width")
    head_index = lax.axis_index("heads")
    width_index = lax.axis_index("width")
    widened = tokens.astype(jnp.float32)
    square_sums = lax.psum(jnp.sum(widened * widened, axis=1), "width")
    normed_inputs = (
        widened
        * lax.rsqrt(square_sums[:, None] / MODEL_WIDTH + 1e-05)
        * norm_gain.astype(jnp.float32)[None, :]
    ).astype(jnp.bfloat16)
    query_cols = w_query.shape[1]
    pair_cols = key_weight_matrix.shape[1]
    all_rows = tokens.shape[0] * head_count
    half_rows = all_rows // width_count
    whole_rows = lax.all_gather(normed_inputs, "heads", axis=0, tiled=True)
    swap = [(i, (i + 1) % width_count) for i in range(width_count)]
    other_rows = lax.ppermute(w_out, "width", swap)
    pair_sum = lax.psum_scatter(
        jnp.concatenate(
            [
                jnp.dot(whole_rows, key_weight_matrix, preferred_element_type=jnp.float32),
                jnp.dot(whole_rows, value_weight_matrix, preferred_element_type=jnp.float32),
            ],
            axis=1,
        ),
        "width",
        scatter_dimension=0,
        tiled=True,
    ).astype(jnp.bfloat16)
    pair_rows = lax.all_gather(pair_sum, "heads", axis=0, tiled=False)
    pair_rows = pair_rows.reshape(head_count, half_rows, 2, pair_cols)
    projected_key_rows = jnp.swapaxes(pair_rows[:, :, 0], 0, 1).reshape(half_rows, -1)
    projected_value_rows = jnp.swapaxes(pair_rows[:, :, 1], 0, 1).reshape(half_rows, -1)
    query_sum = lax.psum_scatter(
        jnp.dot(whole_rows, w_query, preferred_element_type=jnp.float32),
        "width",
        scatter_dimension=0,
        tiled=True,
    )
    local_heads = query_cols // HEAD_WIDTH
    heads_per_group = QUERY_HEADS // KEY_VALUE_HEADS
    heads_sharing_key = max(local_heads // heads_per_group, 1)
    leading_shared_slot = head_index * local_heads // heads_per_group
    prompts_in_group = half_rows // PROMPT_SLOTS
    cosine_table, sine_table = rope_angles(PROMPT_SLOTS, HEAD_WIDTH)
    queries = rotate(
        query_sum.reshape(prompts_in_group, PROMPT_SLOTS, local_heads, HEAD_WIDTH),
        cosine_table,
        sine_table,
    ).astype(jnp.bfloat16)
    key_grid = jnp.swapaxes(
        projected_key_rows.reshape(prompts_in_group, PROMPT_SLOTS, HEAD_WIDTH, KEY_VALUE_HEADS),
        2,
        3,
    )
    value_grid = jnp.swapaxes(
        projected_value_rows.reshape(prompts_in_group, PROMPT_SLOTS, HEAD_WIDTH, KEY_VALUE_HEADS),
        2,
        3,
    )
    key_heads = lax.dynamic_slice_in_dim(key_grid, leading_shared_slot, heads_sharing_key, 2)
    rotated_keys = rotate(key_heads.astype(jnp.float32), cosine_table, sine_table).astype(
        jnp.bfloat16
    )
    value_heads = lax.dynamic_slice_in_dim(value_grid, leading_shared_slot, heads_sharing_key, 2)
    lengths_here = lax.dynamic_slice_in_dim(
        prompt_len, width_index * prompts_in_group, prompts_in_group
    )
    prefixes_here = lax.dynamic_slice_in_dim(
        prefix_len, width_index * prompts_in_group, prompts_in_group
    )
    allowed = allowed_mask(PROMPT_SLOTS, lengths_here[:, None, None], prefixes_here[:, None, None])
    grouped_queries = queries.reshape(
        prompts_in_group,
        PROMPT_SLOTS,
        heads_sharing_key,
        local_heads // heads_sharing_key,
        HEAD_WIDTH,
    )
    scores = jnp.einsum(
        "bqngd,bknd->bngqk", grouped_queries, rotated_keys, preferred_element_type=jnp.float32
    ) / math.sqrt(HEAD_WIDTH)
    scores = jnp.where(allowed[:, None, None], scores, jnp.float32(-1e30))
    row_peak = jnp.max(scores, axis=-1, keepdims=True)
    raised = jnp.exp(scores - row_peak)
    probabilities = (raised / jnp.sum(raised, axis=-1, keepdims=True)).astype(jnp.bfloat16)
    mixture = jnp.einsum(
        "bngqk,bknd->bqngd", probabilities, value_heads, preferred_element_type=jnp.float32
    )
    attended = mixture.astype(jnp.bfloat16).reshape(half_rows, query_cols)
    every_head = lax.all_gather(attended, "heads", axis=1, tiled=True)
    share = w_out.shape[0]
    own_part = lax.dynamic_slice_in_dim(every_head, width_index * share, share, 1)
    other_index = (width_index + 1) % width_count
    other_part = lax.dynamic_slice_in_dim(every_head, other_index * share, share, 1)
    return (
        jnp.dot(own_part, w_out, preferred_element_type=jnp.float32)
        + jnp.dot(other_part, other_rows, preferred_element_type=jnp.float32)
    ).astype(jnp.bfloat16)


def solution(mesh):
    in_specs = (
        P(("groups", "heads"), "width"),
        P("width"),
        P("width", "heads"),
        P("width", "heads"),
        P("width", "heads"),
        P("width", "heads"),
        P("groups"),
        P("groups"),
    )
    out_specs = P(("groups", "width"), "heads")
    return jax.shard_map(
        per_device, mesh=mesh, in_specs=in_specs, out_specs=out_specs, check_vma=False
    )
```

```python
import functools
import math

import jax
import jax.numpy as jnp
from jax import lax
from jax.experimental import pallas as pl
from jax.experimental.pallas import tpu as pltpu
from jax.sharding import PartitionSpec as P

MODEL_WIDTH = 16384
QUERY_HEADS = 128
KEY_VALUE_HEADS = 8
HEAD_WIDTH = 128
PROMPT_SLOTS = 192


def rope_angles(length, head_size):
    half_size = head_size // 2
    indices = jnp.arange(half_size, dtype=jnp.float32)
    frequency = jnp.exp(-(2.0 * indices / head_size) * math.log(500000.0))
    wavelength = 2.0 * math.pi / frequency
    smooth = (8192.0 / wavelength - 1.0) / 3.0
    blended = (1.0 - smooth) * frequency / 8.0 + smooth * frequency
    frequency = jnp.where(
        wavelength < 2048.0, frequency, jnp.where(wavelength > 8192.0, frequency / 8.0, blended)
    )
    positions = jnp.arange(length, dtype=jnp.float32)
    angles = positions[:, None] * frequency[None, :]
    return (jnp.cos(angles), jnp.sin(angles))


def rotate(vectors, cosine_table, sine_table):
    half_size = vectors.shape[-1] // 2
    leading = vectors[..., :half_size]
    trailing = vectors[..., half_size:]
    cosine_wide = cosine_table[:, None, :]
    sine_wide = sine_table[:, None, :]
    return jnp.concatenate(
        [
            leading * cosine_wide - trailing * sine_wide,
            trailing * cosine_wide + leading * sine_wide,
        ],
        axis=-1,
    )


def allowed_mask(length, prompt_length, prefix_length):
    query_slot = jnp.arange(length, dtype=jnp.int32)[:, None]
    key_slot = jnp.arange(length, dtype=jnp.int32)[None, :]
    return (key_slot < prompt_length) & ((key_slot <= query_slot) | (key_slot < prefix_length))


LAYERS = 4
RING_SIZE = 8
ARRIVAL = ((0, 1, 2, 3), (1, 0, 2, 3), (2, 3, 1, 0), (3, 2, 1, 0))
SEQUENCE = ((0, 0), (1, 0), (0, 1), (2, 0), (1, 1), (3, 0), (2, 1), (3, 1))


def layer_at(layer, place):
    found = jnp.int32(ARRIVAL[LAYERS - 1][place])
    for at in range(LAYERS - 1):
        found = jnp.where(layer == at, ARRIVAL[at][place], found)
    return found


def enter(me):
    layer, side = me // 2, me % 2
    barrier = pltpu.get_barrier_semaphore()

    def greet(target):
        pl.semaphore_signal(
            barrier, inc=1, device_id={"heads": target}, device_id_type=pl.DeviceIdType.MESH
        )

    greet(layer * 2 + 1 - side)

    @pl.when(layer < LAYERS - 1)
    def _():
        greet(me + 2)

    @pl.when(layer > 0)
    def _():
        greet(me - 2)

    pl.semaphore_wait(
        barrier,
        1 + jnp.where(layer < LAYERS - 1, 1, 0) + jnp.where(layer > 0, 1, 0),
    )


def copies(me, place, chunk, view, send_sem, recv_sem):
    layer, side = me // 2, me % 2
    block_layer = layer_at(layer, place)
    owner = block_layer * 2 + side
    ref = view(owner, chunk)

    def to(target, way):
        return pltpu.make_async_remote_copy(
            src_ref=ref,
            dst_ref=ref,
            send_sem=send_sem.at[way, place, chunk],
            recv_sem=recv_sem.at[owner, chunk],
            device_id={"heads": target},
            device_id_type=pl.DeviceIdType.MESH,
        )

    return (
        (to(me + 2, 0), jnp.logical_and(block_layer <= layer, layer < LAYERS - 1)),
        (to(me - 2, 1), jnp.logical_and(block_layer >= layer, layer > 0)),
        (to(layer * 2 + 1 - side, 2), None),
    )


def pass_on(me, place, chunk, view, send_sem, recv_sem):
    for copy, holds in copies(me, place, chunk, view, send_sem, recv_sem):
        if holds is None:
            copy.start()
        else:
            pl.when(holds)(copy.start)


def finish(me, chunks, view, send_sem, recv_sem):
    for place in range(LAYERS):
        for chunk in range(chunks):
            for copy, holds in copies(me, place, chunk, view, send_sem, recv_sem):
                if holds is None:
                    copy.wait_send()
                else:
                    pl.when(holds)(copy.wait_send)


def receive(me, step, chunks, view, send_sem, recv_sem):
    layer, side = me // 2, me % 2
    place, other = SEQUENCE[step]
    owner = layer_at(layer, place) * 2 + (1 - side if other else side)
    for chunk in range(chunks):
        if step:
            ref = view(owner, chunk)
            pltpu.make_async_remote_copy(
                src_ref=ref,
                dst_ref=ref,
                send_sem=send_sem.at[2, place, chunk],
                recv_sem=recv_sem.at[owner, chunk],
                device_id={"heads": layer * 2 + 1 - side},
                device_id_type=pl.DeviceIdType.MESH,
            ).wait_recv()
        if not other:
            pass_on(me, place, chunk, view, send_sem, recv_sem)
    return owner


def gather_kernel(chunks, own_ref, all_ref, own_sem, send_sem, recv_sem):
    me = lax.axis_index("heads")
    rows, cols = own_ref.shape
    wide = cols // chunks

    def view(owner, chunk):
        return all_ref.at[pl.ds(pl.multiple_of(owner * rows, rows), rows), pl.ds(chunk * wide, wide)]

    keep = pltpu.make_async_copy(
        own_ref, all_ref.at[pl.ds(pl.multiple_of(me * rows, rows), rows)], own_sem
    )
    keep.start()
    enter(me)
    keep.wait()
    for step in range(RING_SIZE):
        receive(me, step, chunks, view, send_sem, recv_sem)
    finish(me, chunks, view, send_sem, recv_sem)


def gather_rows(block, chunks, collective_id):
    rows, cols = block.shape
    return pl.pallas_call(
        functools.partial(gather_kernel, chunks),
        out_shape=jax.ShapeDtypeStruct((rows * RING_SIZE, cols), block.dtype),
        in_specs=[pl.BlockSpec(memory_space=pltpu.VMEM)],
        out_specs=pl.BlockSpec(memory_space=pltpu.VMEM),
        scratch_shapes=[
            pltpu.SemaphoreType.DMA,
            pltpu.SemaphoreType.DMA((3, LAYERS, chunks)),
            pltpu.SemaphoreType.DMA((RING_SIZE, chunks)),
        ],
        compiler_params=pltpu.CompilerParams(
            collective_id=collective_id, has_side_effects=True, vmem_limit_bytes=24 * 2**20
        ),
    )(block)


WEIGHT_SLOTS = 3


def project_kernel(
    chunks, own_ref, near_ref, far_ref, out_ref,
    held, total, weights, weight_sem, send_sem, recv_sem,
):
    me = lax.axis_index("heads")
    core = lax.axis_index("width")
    layer, side = me // 2, me % 2
    rows, cols = own_ref.shape
    wide = cols // chunks
    per_half = near_ref.shape[0] // cols
    tile = 256

    def view(owner, chunk):
        return held.at[owner, :, pl.ds(chunk * wide, wide)]

    def fetch(step):
        place, other = SEQUENCE[step]
        owner = layer_at(layer, place) * 2 + (1 - side if other else side)
        at = pl.ds(pl.multiple_of((owner % per_half) * cols, cols), cols)
        slot = step % WEIGHT_SLOTS
        near = owner // per_half == core

        @pl.when(near)
        def _():
            pltpu.make_async_copy(near_ref.at[at], weights.at[slot], weight_sem.at[slot]).start()

        @pl.when(jnp.logical_not(near))
        def _():
            pltpu.make_async_copy(far_ref.at[at], weights.at[slot], weight_sem.at[slot]).start()

    for step in range(WEIGHT_SLOTS):
        fetch(step)
    held[me] = own_ref[...]
    enter(me)
    for step in range(RING_SIZE):
        owner = receive(me, step, chunks, view, send_sem, recv_sem)
        slot = step % WEIGHT_SLOTS
        pltpu.make_async_copy(
            near_ref.at[pl.ds(0, cols)], weights.at[slot], weight_sem.at[slot]
        ).wait()

        @pl.loop(0, out_ref.shape[1] // tile)
        def _(n):
            at = pl.ds(pl.multiple_of(n * tile, tile), tile)
            term = jnp.dot(
                held[owner], weights[slot, :, at], preferred_element_type=jnp.float32
            )
            if step == 0:
                total[:, at] = term
            elif step < RING_SIZE - 1:
                total[:, at] += term
            else:
                out_ref[:, at] = (total[:, at] + term).astype(out_ref.dtype)

        if step + WEIGHT_SLOTS < RING_SIZE:
            fetch(step + WEIGHT_SLOTS)
    finish(me, chunks, view, send_sem, recv_sem)


def gather_and_project(block, near, far, chunks, collective_id):
    rows, cols = block.shape
    out_cols = near.shape[1]
    return pl.pallas_call(
        functools.partial(project_kernel, chunks),
        out_shape=jax.ShapeDtypeStruct((rows, out_cols), jnp.bfloat16),
        in_specs=[
            pl.BlockSpec(memory_space=pltpu.VMEM),
            pl.BlockSpec(memory_space=pl.ANY),
            pl.BlockSpec(memory_space=pl.ANY),
        ],
        out_specs=pl.BlockSpec(memory_space=pltpu.VMEM),
        scratch_shapes=[
            pltpu.VMEM((RING_SIZE, rows, cols), block.dtype),
            pltpu.VMEM((rows, out_cols), jnp.float32),
            pltpu.VMEM((WEIGHT_SLOTS, cols, out_cols), near.dtype),
            pltpu.SemaphoreType.DMA((WEIGHT_SLOTS,)),
            pltpu.SemaphoreType.DMA((3, LAYERS, chunks)),
            pltpu.SemaphoreType.DMA((RING_SIZE, chunks)),
        ],
        compiler_params=pltpu.CompilerParams(
            collective_id=collective_id, has_side_effects=True, vmem_limit_bytes=48 * 2**20
        ),
    )(block, near, far)


def per_device(
    tokens,
    norm_gain,
    w_query,
    key_weight_matrix,
    value_weight_matrix,
    w_out,
    prompt_len,
    prefix_len,
):
    head_count = lax.axis_size("heads")
    width_count = lax.axis_size("width")
    head_index = lax.axis_index("heads")
    width_index = lax.axis_index("width")
    widened = tokens.astype(jnp.float32)
    square_sums = lax.psum(jnp.sum(widened * widened, axis=1), "width")
    normed_inputs = (
        widened
        * lax.rsqrt(square_sums[:, None] / MODEL_WIDTH + 1e-05)
        * norm_gain.astype(jnp.float32)[None, :]
    ).astype(jnp.bfloat16)
    query_cols = w_query.shape[1]
    pair_cols = key_weight_matrix.shape[1]
    all_rows = tokens.shape[0] * head_count
    half_rows = all_rows // width_count
    own_kernels = head_count == RING_SIZE and width_count == 2
    if own_kernels:
        whole_rows = gather_rows(normed_inputs, 4, 1)
    else:
        whole_rows = lax.all_gather(normed_inputs, "heads", axis=0, tiled=True)
    swap = [(i, (i + 1) % width_count) for i in range(width_count)]
    other_rows = lax.ppermute(w_out, "width", swap)
    pair_sum = lax.psum_scatter(
        jnp.concatenate(
            [
                jnp.dot(whole_rows, key_weight_matrix, preferred_element_type=jnp.float32),
                jnp.dot(whole_rows, value_weight_matrix, preferred_element_type=jnp.float32),
            ],
            axis=1,
        ),
        "width",
        scatter_dimension=0,
        tiled=True,
    ).astype(jnp.bfloat16)
    if own_kernels:
        pair_rows = gather_rows(pair_sum, 1, 2)
    else:
        pair_rows = lax.all_gather(pair_sum, "heads", axis=0, tiled=False)
    pair_rows = pair_rows.reshape(head_count, half_rows, 2, pair_cols)
    projected_key_rows = jnp.swapaxes(pair_rows[:, :, 0], 0, 1).reshape(half_rows, -1)
    projected_value_rows = jnp.swapaxes(pair_rows[:, :, 1], 0, 1).reshape(half_rows, -1)
    query_sum = lax.psum_scatter(
        jnp.dot(whole_rows, w_query, preferred_element_type=jnp.float32),
        "width",
        scatter_dimension=0,
        tiled=True,
    )
    local_heads = query_cols // HEAD_WIDTH
    heads_per_group = QUERY_HEADS // KEY_VALUE_HEADS
    heads_sharing_key = max(local_heads // heads_per_group, 1)
    leading_shared_slot = head_index * local_heads // heads_per_group
    prompts_in_group = half_rows // PROMPT_SLOTS
    cosine_table, sine_table = rope_angles(PROMPT_SLOTS, HEAD_WIDTH)
    queries = rotate(
        query_sum.reshape(prompts_in_group, PROMPT_SLOTS, local_heads, HEAD_WIDTH),
        cosine_table,
        sine_table,
    ).astype(jnp.bfloat16)
    key_grid = jnp.swapaxes(
        projected_key_rows.reshape(prompts_in_group, PROMPT_SLOTS, HEAD_WIDTH, KEY_VALUE_HEADS),
        2,
        3,
    )
    value_grid = jnp.swapaxes(
        projected_value_rows.reshape(prompts_in_group, PROMPT_SLOTS, HEAD_WIDTH, KEY_VALUE_HEADS),
        2,
        3,
    )
    key_heads = lax.dynamic_slice_in_dim(key_grid, leading_shared_slot, heads_sharing_key, 2)
    rotated_keys = rotate(key_heads.astype(jnp.float32), cosine_table, sine_table).astype(
        jnp.bfloat16
    )
    value_heads = lax.dynamic_slice_in_dim(value_grid, leading_shared_slot, heads_sharing_key, 2)
    lengths_here = lax.dynamic_slice_in_dim(
        prompt_len, width_index * prompts_in_group, prompts_in_group
    )
    prefixes_here = lax.dynamic_slice_in_dim(
        prefix_len, width_index * prompts_in_group, prompts_in_group
    )
    allowed = allowed_mask(PROMPT_SLOTS, lengths_here[:, None, None], prefixes_here[:, None, None])
    grouped_queries = queries.reshape(
        prompts_in_group,
        PROMPT_SLOTS,
        heads_sharing_key,
        local_heads // heads_sharing_key,
        HEAD_WIDTH,
    )
    scores = jnp.einsum(
        "bqngd,bknd->bngqk", grouped_queries, rotated_keys, preferred_element_type=jnp.float32
    ) / math.sqrt(HEAD_WIDTH)
    scores = jnp.where(allowed[:, None, None], scores, jnp.float32(-1e30))
    row_peak = jnp.max(scores, axis=-1, keepdims=True)
    raised = jnp.exp(scores - row_peak)
    probabilities = (raised / jnp.sum(raised, axis=-1, keepdims=True)).astype(jnp.bfloat16)
    mixture = jnp.einsum(
        "bngqk,bknd->bqngd", probabilities, value_heads, preferred_element_type=jnp.float32
    )
    attended = mixture.astype(jnp.bfloat16).reshape(half_rows, query_cols)
    if own_kernels:
        return gather_and_project(attended, w_out, other_rows, 4, 3)
    every_head = lax.all_gather(attended, "heads", axis=1, tiled=True)
    share = w_out.shape[0]
    own_part = lax.dynamic_slice_in_dim(every_head, width_index * share, share, 1)
    other_index = (width_index + 1) % width_count
    other_part = lax.dynamic_slice_in_dim(every_head, other_index * share, share, 1)
    return (
        jnp.dot(own_part, w_out, preferred_element_type=jnp.float32)
        + jnp.dot(other_part, other_rows, preferred_element_type=jnp.float32)
    ).astype(jnp.bfloat16)


def solution(mesh):
    in_specs = (
        P(("groups", "heads"), "width"),
        P("width"),
        P("width", "heads"),
        P("width", "heads"),
        P("width", "heads"),
        P("width", "heads"),
        P("groups"),
        P("groups"),
    )
    out_specs = P(("groups", "width"), "heads")
    return jax.shard_map(
        per_device, mesh=mesh, in_specs=in_specs, out_specs=out_specs, check_vma=False
    )
```

```python
import functools
import math

import jax
import jax.numpy as jnp
from jax import lax
from jax.experimental import pallas as pl
from jax.experimental.pallas import tpu as pltpu
from jax.sharding import PartitionSpec as P

MODEL_WIDTH = 16384
QUERY_HEADS = 128
KEY_VALUE_HEADS = 8
HEAD_WIDTH = 128
PROMPT_SLOTS = 192


def rope_angles(length, head_size):
    half_size = head_size // 2
    indices = jnp.arange(half_size, dtype=jnp.float32)
    frequency = jnp.exp(-(2.0 * indices / head_size) * math.log(500000.0))
    wavelength = 2.0 * math.pi / frequency
    smooth = (8192.0 / wavelength - 1.0) / 3.0
    blended = (1.0 - smooth) * frequency / 8.0 + smooth * frequency
    frequency = jnp.where(
        wavelength < 2048.0, frequency, jnp.where(wavelength > 8192.0, frequency / 8.0, blended)
    )
    positions = jnp.arange(length, dtype=jnp.float32)
    angles = positions[:, None] * frequency[None, :]
    return (jnp.cos(angles), jnp.sin(angles))


def rotate(vectors, cosine_table, sine_table):
    half_size = vectors.shape[-1] // 2
    leading = vectors[..., :half_size]
    trailing = vectors[..., half_size:]
    cosine_wide = cosine_table[:, None, :]
    sine_wide = sine_table[:, None, :]
    return jnp.concatenate(
        [
            leading * cosine_wide - trailing * sine_wide,
            trailing * cosine_wide + leading * sine_wide,
        ],
        axis=-1,
    )


def allowed_mask(length, prompt_length, prefix_length):
    query_slot = jnp.arange(length, dtype=jnp.int32)[:, None]
    key_slot = jnp.arange(length, dtype=jnp.int32)[None, :]
    return (key_slot < prompt_length) & ((key_slot <= query_slot) | (key_slot < prefix_length))


LAYERS = 4
RING_SIZE = 8
ARRIVAL = ((0, 1, 2, 3), (1, 0, 2, 3), (2, 3, 1, 0), (3, 2, 1, 0))
SEQUENCE = ((0, 0), (1, 0), (0, 1), (2, 0), (1, 1), (3, 0), (2, 1), (3, 1))


def layer_at(layer, place):
    found = jnp.int32(ARRIVAL[LAYERS - 1][place])
    for at in range(LAYERS - 1):
        found = jnp.where(layer == at, ARRIVAL[at][place], found)
    return found


def enter(me):
    layer, side = me // 2, me % 2
    barrier = pltpu.get_barrier_semaphore()

    def greet(target):
        pl.semaphore_signal(
            barrier, inc=1, device_id={"heads": target}, device_id_type=pl.DeviceIdType.MESH
        )

    greet(layer * 2 + 1 - side)

    @pl.when(layer < LAYERS - 1)
    def _():
        greet(me + 2)

    @pl.when(layer > 0)
    def _():
        greet(me - 2)

    pl.semaphore_wait(
        barrier,
        1 + jnp.where(layer < LAYERS - 1, 1, 0) + jnp.where(layer > 0, 1, 0),
    )


def copies(me, place, chunk, view, send_sem, recv_sem):
    layer, side = me // 2, me % 2
    block_layer = layer_at(layer, place)
    owner = block_layer * 2 + side
    ref = view(owner, chunk)

    def to(target, way):
        return pltpu.make_async_remote_copy(
            src_ref=ref,
            dst_ref=ref,
            send_sem=send_sem.at[way, place, chunk],
            recv_sem=recv_sem.at[owner, chunk],
            device_id={"heads": target},
            device_id_type=pl.DeviceIdType.MESH,
        )

    return (
        (to(me + 2, 0), jnp.logical_and(block_layer <= layer, layer < LAYERS - 1)),
        (to(me - 2, 1), jnp.logical_and(block_layer >= layer, layer > 0)),
        (to(layer * 2 + 1 - side, 2), None),
    )


def pass_on(me, place, chunk, view, send_sem, recv_sem):
    for copy, holds in copies(me, place, chunk, view, send_sem, recv_sem):
        if holds is None:
            copy.start()
        else:
            pl.when(holds)(copy.start)


def finish(me, chunks, view, send_sem, recv_sem):
    for place in range(LAYERS):
        for chunk in range(chunks):
            for copy, holds in copies(me, place, chunk, view, send_sem, recv_sem):
                if holds is None:
                    copy.wait_send()
                else:
                    pl.when(holds)(copy.wait_send)


def receive(me, step, chunks, view, send_sem, recv_sem):
    layer, side = me // 2, me % 2
    place, other = SEQUENCE[step]
    owner = layer_at(layer, place) * 2 + (1 - side if other else side)
    for chunk in range(chunks):
        if step:
            ref = view(owner, chunk)
            pltpu.make_async_remote_copy(
                src_ref=ref,
                dst_ref=ref,
                send_sem=send_sem.at[2, place, chunk],
                recv_sem=recv_sem.at[owner, chunk],
                device_id={"heads": layer * 2 + 1 - side},
                device_id_type=pl.DeviceIdType.MESH,
            ).wait_recv()
        if not other:
            pass_on(me, place, chunk, view, send_sem, recv_sem)
    return owner


def gather_kernel(chunks, own_ref, all_ref, own_sem, send_sem, recv_sem):
    me = lax.axis_index("heads")
    rows, cols = own_ref.shape
    wide = cols // chunks

    def view(owner, chunk):
        return all_ref.at[pl.ds(pl.multiple_of(owner * rows, rows), rows), pl.ds(chunk * wide, wide)]

    keep = pltpu.make_async_copy(
        own_ref, all_ref.at[pl.ds(pl.multiple_of(me * rows, rows), rows)], own_sem
    )
    keep.start()
    enter(me)
    keep.wait()
    for step in range(RING_SIZE):
        receive(me, step, chunks, view, send_sem, recv_sem)
    finish(me, chunks, view, send_sem, recv_sem)


def gather_rows(block, chunks, collective_id):
    rows, cols = block.shape
    return pl.pallas_call(
        functools.partial(gather_kernel, chunks),
        out_shape=jax.ShapeDtypeStruct((rows * RING_SIZE, cols), block.dtype),
        in_specs=[pl.BlockSpec(memory_space=pltpu.VMEM)],
        out_specs=pl.BlockSpec(memory_space=pltpu.VMEM),
        scratch_shapes=[
            pltpu.SemaphoreType.DMA,
            pltpu.SemaphoreType.DMA((3, LAYERS, chunks)),
            pltpu.SemaphoreType.DMA((RING_SIZE, chunks)),
        ],
        compiler_params=pltpu.CompilerParams(
            collective_id=collective_id, has_side_effects=True, vmem_limit_bytes=24 * 2**20
        ),
    )(block)


WEIGHT_SLOTS = 3


def project_kernel(
    chunks, own_ref, near_ref, far_ref, out_ref,
    held, total, weights, weight_sem, send_sem, recv_sem,
):
    me = lax.axis_index("heads")
    core = lax.axis_index("width")
    layer, side = me // 2, me % 2
    rows, cols = own_ref.shape
    wide = cols // chunks
    per_half = near_ref.shape[0] // cols
    tile = 256

    def view(owner, chunk):
        return held.at[owner, :, pl.ds(chunk * wide, wide)]

    def fetch(step):
        place, other = SEQUENCE[step]
        owner = layer_at(layer, place) * 2 + (1 - side if other else side)
        at = pl.ds(pl.multiple_of((owner % per_half) * cols, cols), cols)
        slot = step % WEIGHT_SLOTS
        near = owner // per_half == core

        @pl.when(near)
        def _():
            pltpu.make_async_copy(near_ref.at[at], weights.at[slot], weight_sem.at[slot]).start()

        @pl.when(jnp.logical_not(near))
        def _():
            pltpu.make_async_copy(far_ref.at[at], weights.at[slot], weight_sem.at[slot]).start()

    for step in range(WEIGHT_SLOTS):
        fetch(step)
    held[me] = own_ref[...]
    enter(me)
    for step in range(RING_SIZE):
        owner = receive(me, step, chunks, view, send_sem, recv_sem)
        slot = step % WEIGHT_SLOTS
        pltpu.make_async_copy(
            near_ref.at[pl.ds(0, cols)], weights.at[slot], weight_sem.at[slot]
        ).wait()

        @pl.loop(0, out_ref.shape[1] // tile)
        def _(n):
            at = pl.ds(pl.multiple_of(n * tile, tile), tile)
            term = jnp.dot(
                held[owner], weights[slot, :, at], preferred_element_type=jnp.float32
            )
            if step == 0:
                total[:, at] = term
            elif step < RING_SIZE - 1:
                total[:, at] += term
            else:
                out_ref[:, at] = (total[:, at] + term).astype(out_ref.dtype)

        if step + WEIGHT_SLOTS < RING_SIZE:
            fetch(step + WEIGHT_SLOTS)
    finish(me, chunks, view, send_sem, recv_sem)


def gather_and_project(block, near, far, chunks, collective_id):
    rows, cols = block.shape
    out_cols = near.shape[1]
    return pl.pallas_call(
        functools.partial(project_kernel, chunks),
        out_shape=jax.ShapeDtypeStruct((rows, out_cols), jnp.bfloat16),
        in_specs=[
            pl.BlockSpec(memory_space=pltpu.VMEM),
            pl.BlockSpec(memory_space=pl.ANY),
            pl.BlockSpec(memory_space=pl.ANY),
        ],
        out_specs=pl.BlockSpec(memory_space=pltpu.VMEM),
        scratch_shapes=[
            pltpu.VMEM((RING_SIZE, rows, cols), block.dtype),
            pltpu.VMEM((rows, out_cols), jnp.float32),
            pltpu.VMEM((WEIGHT_SLOTS, cols, out_cols), near.dtype),
            pltpu.SemaphoreType.DMA((WEIGHT_SLOTS,)),
            pltpu.SemaphoreType.DMA((3, LAYERS, chunks)),
            pltpu.SemaphoreType.DMA((RING_SIZE, chunks)),
        ],
        compiler_params=pltpu.CompilerParams(
            collective_id=collective_id, has_side_effects=True, vmem_limit_bytes=48 * 2**20
        ),
    )(block, near, far)


def per_device(
    tokens,
    norm_gain,
    w_query,
    key_weight_matrix,
    value_weight_matrix,
    w_out,
    prompt_len,
    prefix_len,
):
    head_count = lax.axis_size("heads")
    width_count = lax.axis_size("width")
    head_index = lax.axis_index("heads")
    width_index = lax.axis_index("width")
    widened = tokens.astype(jnp.float32)
    square_sums = lax.psum(jnp.sum(widened * widened, axis=1), "width")
    square_sums, late_rows = lax.optimization_barrier((square_sums, w_out))
    swap = [(i, (i + 1) % width_count) for i in range(width_count)]
    other_rows = lax.ppermute(late_rows, "width", swap)
    normed_inputs = (
        widened
        * lax.rsqrt(square_sums[:, None] / MODEL_WIDTH + 1e-05)
        * norm_gain.astype(jnp.float32)[None, :]
    ).astype(jnp.bfloat16)
    query_cols = w_query.shape[1]
    pair_cols = key_weight_matrix.shape[1]
    all_rows = tokens.shape[0] * head_count
    half_rows = all_rows // width_count
    own_kernels = head_count == RING_SIZE and width_count == 2
    if own_kernels:
        whole_rows = gather_rows(normed_inputs, 8, 1)
    else:
        whole_rows = lax.all_gather(normed_inputs, "heads", axis=0, tiled=True)
    pair_sum = lax.psum_scatter(
        jnp.concatenate(
            [
                jnp.dot(whole_rows, key_weight_matrix, preferred_element_type=jnp.float32),
                jnp.dot(whole_rows, value_weight_matrix, preferred_element_type=jnp.float32),
            ],
            axis=1,
        ),
        "width",
        scatter_dimension=0,
        tiled=True,
    ).astype(jnp.bfloat16)
    if own_kernels:
        pair_rows = gather_rows(pair_sum, 1, 2)
    else:
        pair_rows = lax.all_gather(pair_sum, "heads", axis=0, tiled=False)
    pair_rows = pair_rows.reshape(head_count, half_rows, 2, pair_cols)
    projected_key_rows = jnp.swapaxes(pair_rows[:, :, 0], 0, 1).reshape(half_rows, -1)
    projected_value_rows = jnp.swapaxes(pair_rows[:, :, 1], 0, 1).reshape(half_rows, -1)
    query_sum = lax.psum_scatter(
        jnp.dot(whole_rows, w_query, preferred_element_type=jnp.float32),
        "width",
        scatter_dimension=0,
        tiled=True,
    )
    local_heads = query_cols // HEAD_WIDTH
    heads_per_group = QUERY_HEADS // KEY_VALUE_HEADS
    heads_sharing_key = max(local_heads // heads_per_group, 1)
    leading_shared_slot = head_index * local_heads // heads_per_group
    prompts_in_group = half_rows // PROMPT_SLOTS
    cosine_table, sine_table = rope_angles(PROMPT_SLOTS, HEAD_WIDTH)
    queries = rotate(
        query_sum.reshape(prompts_in_group, PROMPT_SLOTS, local_heads, HEAD_WIDTH),
        cosine_table,
        sine_table,
    ).astype(jnp.bfloat16)
    key_grid = jnp.swapaxes(
        projected_key_rows.reshape(prompts_in_group, PROMPT_SLOTS, HEAD_WIDTH, KEY_VALUE_HEADS),
        2,
        3,
    )
    value_grid = jnp.swapaxes(
        projected_value_rows.reshape(prompts_in_group, PROMPT_SLOTS, HEAD_WIDTH, KEY_VALUE_HEADS),
        2,
        3,
    )
    key_heads = lax.dynamic_slice_in_dim(key_grid, leading_shared_slot, heads_sharing_key, 2)
    rotated_keys = rotate(key_heads.astype(jnp.float32), cosine_table, sine_table).astype(
        jnp.bfloat16
    )
    value_heads = lax.dynamic_slice_in_dim(value_grid, leading_shared_slot, heads_sharing_key, 2)
    lengths_here = lax.dynamic_slice_in_dim(
        prompt_len, width_index * prompts_in_group, prompts_in_group
    )
    prefixes_here = lax.dynamic_slice_in_dim(
        prefix_len, width_index * prompts_in_group, prompts_in_group
    )
    allowed = allowed_mask(PROMPT_SLOTS, lengths_here[:, None, None], prefixes_here[:, None, None])
    grouped_queries = queries.reshape(
        prompts_in_group,
        PROMPT_SLOTS,
        heads_sharing_key,
        local_heads // heads_sharing_key,
        HEAD_WIDTH,
    )
    scores = jnp.einsum(
        "bqngd,bknd->bngqk", grouped_queries, rotated_keys, preferred_element_type=jnp.float32
    ) / math.sqrt(HEAD_WIDTH)
    scores = jnp.where(allowed[:, None, None], scores, jnp.float32(-1e30))
    row_peak = jnp.max(scores, axis=-1, keepdims=True)
    raised = jnp.exp(scores - row_peak)
    probabilities = (raised / jnp.sum(raised, axis=-1, keepdims=True)).astype(jnp.bfloat16)
    mixture = jnp.einsum(
        "bngqk,bknd->bqngd", probabilities, value_heads, preferred_element_type=jnp.float32
    )
    attended = mixture.astype(jnp.bfloat16).reshape(half_rows, query_cols)
    if own_kernels:
        return gather_and_project(attended, w_out, other_rows, 8, 3)
    every_head = lax.all_gather(attended, "heads", axis=1, tiled=True)
    share = w_out.shape[0]
    own_part = lax.dynamic_slice_in_dim(every_head, width_index * share, share, 1)
    other_index = (width_index + 1) % width_count
    other_part = lax.dynamic_slice_in_dim(every_head, other_index * share, share, 1)
    return (
        jnp.dot(own_part, w_out, preferred_element_type=jnp.float32)
        + jnp.dot(other_part, other_rows, preferred_element_type=jnp.float32)
    ).astype(jnp.bfloat16)


def solution(mesh):
    in_specs = (
        P(("groups", "heads"), "width"),
        P("width"),
        P("width", "heads"),
        P("width", "heads"),
        P("width", "heads"),
        P("width", "heads"),
        P("groups"),
        P("groups"),
    )
    out_specs = P(("groups", "width"), "heads")
    return jax.shard_map(
        per_device, mesh=mesh, in_specs=in_specs, out_specs=out_specs, check_vma=False
    )
```

```python
import functools
import math

import jax
import jax.numpy as jnp
from jax import lax
from jax.experimental import pallas as pl
from jax.experimental.pallas import tpu as pltpu
from jax.sharding import PartitionSpec as P

MODEL_WIDTH = 16384
QUERY_HEADS = 128
KEY_VALUE_HEADS = 8
HEAD_WIDTH = 128
PROMPT_SLOTS = 192


def rope_angles(length, head_size):
    half_size = head_size // 2
    indices = jnp.arange(half_size, dtype=jnp.float32)
    frequency = jnp.exp(-(2.0 * indices / head_size) * math.log(500000.0))
    wavelength = 2.0 * math.pi / frequency
    smooth = (8192.0 / wavelength - 1.0) / 3.0
    blended = (1.0 - smooth) * frequency / 8.0 + smooth * frequency
    frequency = jnp.where(
        wavelength < 2048.0, frequency, jnp.where(wavelength > 8192.0, frequency / 8.0, blended)
    )
    positions = jnp.arange(length, dtype=jnp.float32)
    angles = positions[:, None] * frequency[None, :]
    return (jnp.cos(angles), jnp.sin(angles))


def rotate(vectors, cosine_table, sine_table):
    half_size = vectors.shape[-1] // 2
    leading = vectors[..., :half_size]
    trailing = vectors[..., half_size:]
    cosine_wide = cosine_table[:, None, :]
    sine_wide = sine_table[:, None, :]
    return jnp.concatenate(
        [
            leading * cosine_wide - trailing * sine_wide,
            trailing * cosine_wide + leading * sine_wide,
        ],
        axis=-1,
    )


def allowed_mask(length, prompt_length, prefix_length):
    query_slot = jnp.arange(length, dtype=jnp.int32)[:, None]
    key_slot = jnp.arange(length, dtype=jnp.int32)[None, :]
    return (key_slot < prompt_length) & ((key_slot <= query_slot) | (key_slot < prefix_length))


LAYERS = 4
RING_SIZE = 8
ARRIVAL = ((0, 1, 2, 3), (1, 0, 2, 3), (2, 3, 1, 0), (3, 2, 1, 0))
SEQUENCE = ((0, 0), (1, 0), (0, 1), (2, 0), (1, 1), (3, 0), (2, 1), (3, 1))


def layer_at(layer, place):
    found = jnp.int32(ARRIVAL[LAYERS - 1][place])
    for at in range(LAYERS - 1):
        found = jnp.where(layer == at, ARRIVAL[at][place], found)
    return found


def enter(me):
    layer, side = me // 2, me % 2
    barrier = pltpu.get_barrier_semaphore()

    def greet(target):
        pl.semaphore_signal(
            barrier, inc=1, device_id={"heads": target}, device_id_type=pl.DeviceIdType.MESH
        )

    greet(layer * 2 + 1 - side)

    @pl.when(layer < LAYERS - 1)
    def _():
        greet(me + 2)

    @pl.when(layer > 0)
    def _():
        greet(me - 2)

    pl.semaphore_wait(
        barrier,
        1 + jnp.where(layer < LAYERS - 1, 1, 0) + jnp.where(layer > 0, 1, 0),
    )


def copies(me, place, chunk, view, send_sem, recv_sem):
    layer, side = me // 2, me % 2
    block_layer = layer_at(layer, place)
    owner = block_layer * 2 + side
    ref = view(owner, chunk)

    def to(target, way):
        return pltpu.make_async_remote_copy(
            src_ref=ref,
            dst_ref=ref,
            send_sem=send_sem.at[way, place, chunk],
            recv_sem=recv_sem.at[owner, chunk],
            device_id={"heads": target},
            device_id_type=pl.DeviceIdType.MESH,
        )

    return (
        (to(me + 2, 0), jnp.logical_and(block_layer <= layer, layer < LAYERS - 1)),
        (to(me - 2, 1), jnp.logical_and(block_layer >= layer, layer > 0)),
        (to(layer * 2 + 1 - side, 2), None),
    )


def pass_on(me, place, chunk, view, send_sem, recv_sem):
    for copy, holds in copies(me, place, chunk, view, send_sem, recv_sem):
        if holds is None:
            copy.start()
        else:
            pl.when(holds)(copy.start)


def finish(me, chunks, view, send_sem, recv_sem):
    for place in range(LAYERS):
        for chunk in range(chunks):
            for copy, holds in copies(me, place, chunk, view, send_sem, recv_sem):
                if holds is None:
                    copy.wait_send()
                else:
                    pl.when(holds)(copy.wait_send)


def receive(me, step, chunks, view, send_sem, recv_sem):
    layer, side = me // 2, me % 2
    place, other = SEQUENCE[step]
    owner = layer_at(layer, place) * 2 + (1 - side if other else side)
    for chunk in range(chunks):
        if step:
            ref = view(owner, chunk)
            pltpu.make_async_remote_copy(
                src_ref=ref,
                dst_ref=ref,
                send_sem=send_sem.at[2, place, chunk],
                recv_sem=recv_sem.at[owner, chunk],
                device_id={"heads": layer * 2 + 1 - side},
                device_id_type=pl.DeviceIdType.MESH,
            ).wait_recv()
        if not other:
            pass_on(me, place, chunk, view, send_sem, recv_sem)
    return owner


def gather_kernel(chunks, own_ref, all_ref, own_sem, send_sem, recv_sem):
    me = lax.axis_index("heads")
    rows, cols = own_ref.shape
    wide = cols // chunks

    def view(owner, chunk):
        return all_ref.at[pl.ds(pl.multiple_of(owner * rows, rows), rows), pl.ds(chunk * wide, wide)]

    keep = pltpu.make_async_copy(
        own_ref, all_ref.at[pl.ds(pl.multiple_of(me * rows, rows), rows)], own_sem
    )
    keep.start()
    enter(me)
    keep.wait()
    for step in range(RING_SIZE):
        receive(me, step, chunks, view, send_sem, recv_sem)
    finish(me, chunks, view, send_sem, recv_sem)


def gather_rows(block, chunks, collective_id):
    rows, cols = block.shape
    return pl.pallas_call(
        functools.partial(gather_kernel, chunks),
        out_shape=jax.ShapeDtypeStruct((rows * RING_SIZE, cols), block.dtype),
        in_specs=[pl.BlockSpec(memory_space=pltpu.VMEM)],
        out_specs=pl.BlockSpec(memory_space=pltpu.VMEM),
        scratch_shapes=[
            pltpu.SemaphoreType.DMA,
            pltpu.SemaphoreType.DMA((3, LAYERS, chunks)),
            pltpu.SemaphoreType.DMA((RING_SIZE, chunks)),
        ],
        compiler_params=pltpu.CompilerParams(
            collective_id=collective_id, has_side_effects=True, vmem_limit_bytes=24 * 2**20
        ),
    )(block)


def trade_kernel(give_ref, take_ref, own_sem, send_sem, recv_sem):
    me = lax.axis_index("heads")
    barrier = pltpu.get_barrier_semaphore()
    keep = pltpu.make_async_copy(give_ref.at[me], take_ref.at[me], own_sem)
    keep.start()
    for offset in range(1, RING_SIZE):
        pl.semaphore_signal(
            barrier,
            inc=1,
            device_id={"heads": (me + offset) % RING_SIZE},
            device_id_type=pl.DeviceIdType.MESH,
        )
    pl.semaphore_wait(barrier, RING_SIZE - 1)

    def trade(offset, source_ref, target_ref):
        return pltpu.make_async_remote_copy(
            src_ref=source_ref,
            dst_ref=target_ref,
            send_sem=send_sem.at[offset - 1],
            recv_sem=recv_sem.at[offset - 1],
            device_id={"heads": (me + offset) % RING_SIZE},
            device_id_type=pl.DeviceIdType.MESH,
        )

    for offset in range(1, RING_SIZE):
        peer = (me + offset) % RING_SIZE
        trade(offset, give_ref.at[peer], take_ref.at[me]).start()
    keep.wait()
    for offset in range(1, RING_SIZE):
        source = (me + RING_SIZE - offset) % RING_SIZE
        trade(offset, give_ref.at[source], take_ref.at[source]).wait_recv()
    for offset in range(1, RING_SIZE):
        peer = (me + offset) % RING_SIZE
        trade(offset, give_ref.at[peer], take_ref.at[me]).wait_send()


def trade_blocks(blocks, collective_id):
    return pl.pallas_call(
        trade_kernel,
        out_shape=jax.ShapeDtypeStruct(blocks.shape, blocks.dtype),
        in_specs=[pl.BlockSpec(memory_space=pltpu.VMEM)],
        out_specs=pl.BlockSpec(memory_space=pltpu.VMEM),
        scratch_shapes=[
            pltpu.SemaphoreType.DMA,
            pltpu.SemaphoreType.DMA((RING_SIZE - 1,)),
            pltpu.SemaphoreType.DMA((RING_SIZE - 1,)),
        ],
        compiler_params=pltpu.CompilerParams(collective_id=collective_id, has_side_effects=True),
    )(blocks)


WEIGHT_SLOTS = 3


def project_kernel(
    chunks, own_ref, near_ref, far_ref, out_ref,
    held, total, weights, weight_sem, send_sem, recv_sem,
):
    me = lax.axis_index("heads")
    core = lax.axis_index("width")
    layer, side = me // 2, me % 2
    rows, cols = own_ref.shape
    wide = cols // chunks
    per_half = near_ref.shape[0] // cols
    tile = 256

    def view(owner, chunk):
        return held.at[owner, :, pl.ds(chunk * wide, wide)]

    def fetch(step):
        place, other = SEQUENCE[step]
        owner = layer_at(layer, place) * 2 + (1 - side if other else side)
        at = pl.ds(pl.multiple_of((owner % per_half) * cols, cols), cols)
        slot = step % WEIGHT_SLOTS
        near = owner // per_half == core

        @pl.when(near)
        def _():
            pltpu.make_async_copy(near_ref.at[at], weights.at[slot], weight_sem.at[slot]).start()

        @pl.when(jnp.logical_not(near))
        def _():
            pltpu.make_async_copy(far_ref.at[at], weights.at[slot], weight_sem.at[slot]).start()

    for step in range(WEIGHT_SLOTS):
        fetch(step)
    held[me] = own_ref[...]
    enter(me)
    for step in range(RING_SIZE):
        owner = receive(me, step, chunks, view, send_sem, recv_sem)
        slot = step % WEIGHT_SLOTS
        pltpu.make_async_copy(
            near_ref.at[pl.ds(0, cols)], weights.at[slot], weight_sem.at[slot]
        ).wait()

        @pl.loop(0, out_ref.shape[1] // tile)
        def _(n):
            at = pl.ds(pl.multiple_of(n * tile, tile), tile)
            term = jnp.dot(
                held[owner], weights[slot, :, at], preferred_element_type=jnp.float32
            )
            if step == 0:
                total[:, at] = term
            elif step < RING_SIZE - 1:
                total[:, at] += term
            else:
                out_ref[:, at] = (total[:, at] + term).astype(out_ref.dtype)

        if step + WEIGHT_SLOTS < RING_SIZE:
            fetch(step + WEIGHT_SLOTS)
    finish(me, chunks, view, send_sem, recv_sem)


def gather_and_project(block, near, far, chunks, collective_id):
    rows, cols = block.shape
    out_cols = near.shape[1]
    return pl.pallas_call(
        functools.partial(project_kernel, chunks),
        out_shape=jax.ShapeDtypeStruct((rows, out_cols), jnp.bfloat16),
        in_specs=[
            pl.BlockSpec(memory_space=pltpu.VMEM),
            pl.BlockSpec(memory_space=pl.ANY),
            pl.BlockSpec(memory_space=pl.ANY),
        ],
        out_specs=pl.BlockSpec(memory_space=pltpu.VMEM),
        scratch_shapes=[
            pltpu.VMEM((RING_SIZE, rows, cols), block.dtype),
            pltpu.VMEM((rows, out_cols), jnp.float32),
            pltpu.VMEM((WEIGHT_SLOTS, cols, out_cols), near.dtype),
            pltpu.SemaphoreType.DMA((WEIGHT_SLOTS,)),
            pltpu.SemaphoreType.DMA((3, LAYERS, chunks)),
            pltpu.SemaphoreType.DMA((RING_SIZE, chunks)),
        ],
        compiler_params=pltpu.CompilerParams(
            collective_id=collective_id, has_side_effects=True, vmem_limit_bytes=48 * 2**20
        ),
    )(block, near, far)


def per_device(
    tokens,
    norm_gain,
    w_query,
    key_weight_matrix,
    value_weight_matrix,
    w_out,
    prompt_len,
    prefix_len,
):
    head_count = lax.axis_size("heads")
    width_count = lax.axis_size("width")
    head_index = lax.axis_index("heads")
    width_index = lax.axis_index("width")
    widened = tokens.astype(jnp.float32)
    square_sums = lax.psum(jnp.sum(widened * widened, axis=1), "width")
    square_sums, late_rows = lax.optimization_barrier((square_sums, w_out))
    swap = [(i, (i + 1) % width_count) for i in range(width_count)]
    other_rows = lax.ppermute(late_rows, "width", swap)
    normed_inputs = (
        widened
        * lax.rsqrt(square_sums[:, None] / MODEL_WIDTH + 1e-05)
        * norm_gain.astype(jnp.float32)[None, :]
    ).astype(jnp.bfloat16)
    query_cols = w_query.shape[1]
    pair_cols = key_weight_matrix.shape[1]
    all_rows = tokens.shape[0] * head_count
    half_rows = all_rows // width_count
    own_kernels = head_count == RING_SIZE and width_count == 2
    if own_kernels:
        whole_rows = gather_rows(normed_inputs, 8, 1)
    else:
        whole_rows = lax.all_gather(normed_inputs, "heads", axis=0, tiled=True)
    pair_sum = lax.psum_scatter(
        jnp.concatenate(
            [
                jnp.dot(whole_rows, key_weight_matrix, preferred_element_type=jnp.float32),
                jnp.dot(whole_rows, value_weight_matrix, preferred_element_type=jnp.float32),
            ],
            axis=1,
        ),
        "width",
        scatter_dimension=0,
        tiled=True,
    ).astype(jnp.bfloat16)
    if own_kernels:
        piece = pair_cols // KEY_VALUE_HEADS
        blocks = pair_sum.reshape(half_rows, 2 * piece, KEY_VALUE_HEADS).transpose(2, 1, 0)
        traded = trade_blocks(blocks, 2).reshape(head_count, 2, piece, half_rows)
        traded = traded.transpose(1, 3, 0, 2).reshape(2, -1, PROMPT_SLOTS, 1, HEAD_WIDTH)
    else:
        pair_rows = lax.all_gather(pair_sum, "heads", axis=0, tiled=False)
        pair_rows = pair_rows.reshape(head_count, half_rows, 2, pair_cols)
        projected_key_rows = jnp.swapaxes(pair_rows[:, :, 0], 0, 1).reshape(half_rows, -1)
        projected_value_rows = jnp.swapaxes(pair_rows[:, :, 1], 0, 1).reshape(half_rows, -1)
    query_sum = lax.psum_scatter(
        jnp.dot(whole_rows, w_query, preferred_element_type=jnp.float32),
        "width",
        scatter_dimension=0,
        tiled=True,
    )
    local_heads = query_cols // HEAD_WIDTH
    heads_per_group = QUERY_HEADS // KEY_VALUE_HEADS
    heads_sharing_key = max(local_heads // heads_per_group, 1)
    leading_shared_slot = head_index * local_heads // heads_per_group
    prompts_in_group = half_rows // PROMPT_SLOTS
    cosine_table, sine_table = rope_angles(PROMPT_SLOTS, HEAD_WIDTH)
    queries = rotate(
        query_sum.reshape(prompts_in_group, PROMPT_SLOTS, local_heads, HEAD_WIDTH),
        cosine_table,
        sine_table,
    ).astype(jnp.bfloat16)
    if own_kernels:
        key_heads, value_heads = traded[0], traded[1]
    else:
        key_grid = jnp.swapaxes(
            projected_key_rows.reshape(prompts_in_group, PROMPT_SLOTS, HEAD_WIDTH, KEY_VALUE_HEADS),
            2,
            3,
        )
        value_grid = jnp.swapaxes(
            projected_value_rows.reshape(prompts_in_group, PROMPT_SLOTS, HEAD_WIDTH, KEY_VALUE_HEADS),
            2,
            3,
        )
        key_heads = lax.dynamic_slice_in_dim(key_grid, leading_shared_slot, heads_sharing_key, 2)
        value_heads = lax.dynamic_slice_in_dim(value_grid, leading_shared_slot, heads_sharing_key, 2)
    rotated_keys = rotate(key_heads.astype(jnp.float32), cosine_table, sine_table).astype(
        jnp.bfloat16
    )
    lengths_here = lax.dynamic_slice_in_dim(
        prompt_len, width_index * prompts_in_group, prompts_in_group
    )
    prefixes_here = lax.dynamic_slice_in_dim(
        prefix_len, width_index * prompts_in_group, prompts_in_group
    )
    allowed = allowed_mask(PROMPT_SLOTS, lengths_here[:, None, None], prefixes_here[:, None, None])
    grouped_queries = queries.reshape(
        prompts_in_group,
        PROMPT_SLOTS,
        heads_sharing_key,
        local_heads // heads_sharing_key,
        HEAD_WIDTH,
    )
    scores = jnp.einsum(
        "bqngd,bknd->bngqk", grouped_queries, rotated_keys, preferred_element_type=jnp.float32
    ) / math.sqrt(HEAD_WIDTH)
    scores = jnp.where(allowed[:, None, None], scores, jnp.float32(-1e30))
    row_peak = jnp.max(scores, axis=-1, keepdims=True)
    raised = jnp.exp(scores - row_peak)
    probabilities = (raised / jnp.sum(raised, axis=-1, keepdims=True)).astype(jnp.bfloat16)
    mixture = jnp.einsum(
        "bngqk,bknd->bqngd", probabilities, value_heads, preferred_element_type=jnp.float32
    )
    attended = mixture.astype(jnp.bfloat16).reshape(half_rows, query_cols)
    if own_kernels:
        return gather_and_project(attended, w_out, other_rows, 8, 3)
    every_head = lax.all_gather(attended, "heads", axis=1, tiled=True)
    share = w_out.shape[0]
    own_part = lax.dynamic_slice_in_dim(every_head, width_index * share, share, 1)
    other_index = (width_index + 1) % width_count
    other_part = lax.dynamic_slice_in_dim(every_head, other_index * share, share, 1)
    return (
        jnp.dot(own_part, w_out, preferred_element_type=jnp.float32)
        + jnp.dot(other_part, other_rows, preferred_element_type=jnp.float32)
    ).astype(jnp.bfloat16)


def solution(mesh):
    in_specs = (
        P(("groups", "heads"), "width"),
        P("width"),
        P("width", "heads"),
        P("width", "heads"),
        P("width", "heads"),
        P("width", "heads"),
        P("groups"),
        P("groups"),
    )
    out_specs = P(("groups", "width"), "heads")
    return jax.shard_map(
        per_device, mesh=mesh, in_specs=in_specs, out_specs=out_specs, check_vma=False
    )
```
